32 devices in a mesh: groups: 2 (over y), ep: 8 (over z, x), hg: 2 (over core).
Axes of the slice: x: 2, y: 2, z: 4, core: 2. Of those that a mesh axis runs over, the one named last changes fastest.
Arguments:
- tokens: bfloat16 [64, 3584], P(('groups', 'ep')), parts along dimension 0, may hold values from -6 to 6
- norm_gain: float32 [3584], replicated, may hold values from 0.1 to 1.9
- route_scores: float32 [64, 8], P(('groups', 'ep')), parts along dimension 0, may hold values from 0.02 to 1
- expert_ids: int32 [64, 8], P(('groups', 'ep')), parts along dimension 0, may hold values from 0 to 15, all different within a row; in each aligned block of 2 rows (0 to 1, 2 to 3, ...) at most 2 rows name the same one
- gate_weight: bfloat16 [3584, 32768], P(None, ('ep', 'hg')), may hold values from -0.09375 to 0.09375
- up_weight: bfloat16 [3584, 32768], P(None, ('ep', 'hg')), may hold values from -0.09375 to 0.09375
- down_weight: bfloat16 [32768, 3584], P(('ep', 'hg')), may hold values from -0.125 to 0.125
Outputs:
- mixed: bfloat16 [64, 3584], P(('groups', 'ep'), 'hg'), parts along dimension 0
The draws below stay inside these ranges and needn't reach their ends.
There are 2 independent parts, one for each index of `groups`. The reference program is written for one: setup_inputs(seed, part) draws one part's arguments, and reference() takes and returns one part's arrays. A program takes and returns all parts, laid end to end along the dimension named above; an argument that names none is the same for every part. Nothing has to cross between parts.
Inputs may be any that keep to these rules, and one draw needn't show every extreme that they name: `expert_ids`: each token names 8 different experts. Token rows are laid out by ep index, then micro-batch, then row; in each micro-batch of one ep index (aligned blocks of 2 rows) no expert is named by more than 2 tokens, and in every draw some expert is named by exactly 2 tokens of some block.
All inputs are finite; a program needn't handle non-finite values.
Results may differ from the reference program's by a relative error of at most 0.0055.
Values may be sent and summed in bfloat16 or wider, within the bound.
A program may use at most 128 MiB of HBM per device.

```python
import math
import jax
import jax.numpy as jnp
import numpy as np
from jax import lax

D = 3584
FF = 2048
EXPERTS = 16
TOP = 8
ROWS = 2
CAP = 2
TOKENS = 32
N_EP = 8
N_HG = 2


def block_scale(stream_key, extent, cuts, least, largest):
    level = 1.0
    for dim, shards_of in cuts:
        steps = jax.random.uniform(jax.random.fold_in(jax.random.fold_in(stream_key, 6), dim), (shards_of,), jnp.float32, least / len(cuts), largest / len(cuts))
        level = level * jnp.repeat(jnp.exp(steps), extent[dim] // shards_of).reshape((-1,) + (1,) * (len(extent) - 1 - dim))
    return level


def deal_out(own_key, own, number, rows, number_of, top, bound, lean):
    ranking = jax.random.permutation(own_key, number_of)
    packed, common = shares(number_of, rows * top, bound, lean, True), shares(number_of, rows * top, bound, lean, False)
    places = jnp.arange(number_of)

    def named(lengths, rotation):
        used = int((lengths > 0).sum())
        fixed = max(1, used // 4)
        moved = fixed + (places - fixed + rotation * (used - fixed)) % max(1, number_of - fixed)
        return jnp.zeros((number_of,), jnp.int32).at[ranking[jnp.where(places < fixed, places, moved)]].set(jnp.asarray(lengths, jnp.int32))

    lengths = jnp.where(number % 4 == 0, named(packed, number // 4), named(common, number - number // 4 - 1))
    mixed = jax.random.permutation(jax.random.fold_in(own, 3), number_of)
    giver, receiver = mixed[0:number_of // 2 * 2:2], mixed[1:number_of // 2 * 2:2]
    slack = jnp.minimum(lengths[giver] - 1, bound - lengths[receiver]) // 2
    slack = jnp.where((giver == ranking[0]) | (receiver == ranking[0]) | (lengths[receiver] == 0), 0, jnp.maximum(slack, 0))
    moved = jax.random.randint(jax.random.fold_in(own, 4), (number_of // 2,), 0, 1 << 20) % (slack + 1)
    lengths = lengths.at[giver].add(-moved).at[receiver].add(moved)
    members = jnp.searchsorted(jnp.cumsum(lengths), jnp.arange(rows * top), side="right").astype(jnp.int32)
    grid = members.reshape(top, rows).T
    grid = grid[jax.random.permutation(jax.random.fold_in(own, 1), rows)]
    rotation = jax.random.randint(jax.random.fold_in(own, 2), (rows, 1), 0, top)
    return jnp.take_along_axis(grid, (jnp.arange(top)[None, :] + rotation) % top, axis=1)


def shares(amount, total, limit, skew, full):
    portions = [(1 << 20) // math.isqrt(rank ** skew) + 1 for rank in range(1, amount + 1)]
    largest = limit if full else min(limit, max(-(-total // amount), total * portions[0] // sum(portions)))
    least = 1 if total - largest >= amount - 1 else 0
    counts, rest = [largest] + [least] * (amount - 1), total - largest - least * (amount - 1)
    while rest > 0:
        movable = [i for i in range(1, amount) if counts[i] < largest] or [i for i in range(1, amount) if counts[i] < limit]
        mass, remaining = sum([portions[i] for i in movable]), rest
        for i in movable:
            more = min(limit - counts[i], max(1, remaining * portions[i] // mass), rest)
            counts[i] = counts[i] + more
            rest = rest - more
    return np.array(counts)


def noise(own_key, extent, scale, limit, shards=(), held_as=jnp.bfloat16):
    drawn = scale * jax.random.normal(own_key, extent, jnp.float32)
    if shards:
        drawn = drawn * block_scale(own_key, extent, shards, -0.22, 0.18)
    return jnp.clip(drawn, -limit, limit).astype(held_as)


def setup_inputs(seed: int = 0, part: int = 0) -> dict:
    keys = jax.random.split(jax.random.key(seed), 8)
    part_keys = jax.random.split(jax.random.fold_in(keys[7], part), 8)
    tokens = noise(part_keys[0], (TOKENS, D), 1.0, 6.0, ((0, 8),))
    norm_gain = jnp.clip(1.0 + 0.18 * jax.random.normal(keys[1], (D,), jnp.float32), 0.1, 1.9)
    route_scores = jnp.clip(jnp.exp(math.log(1.0) - 3.912023 * jax.random.uniform(part_keys[2], (TOKENS, TOP), jnp.float32) ** block_scale(part_keys[2], (TOKENS, TOP), ((0, 8),), -0.2, 0.2)), 0.02, 1.0)
    expert_ids_keys = jax.random.split(jax.random.fold_in(part_keys[3], 1), TOKENS // ROWS)
    expert_ids_turns = jax.random.permutation(jax.random.fold_in(part_keys[3], 3), TOKENS // ROWS)
    expert_ids = jax.vmap(lambda own, number: deal_out(jax.random.fold_in(part_keys[3], 2), own, number, ROWS, EXPERTS, TOP, CAP, 2))(expert_ids_keys, expert_ids_turns).reshape((TOKENS, TOP))
    gate_weight = noise(keys[4], (D, EXPERTS * FF), D ** -0.5, 0.09375, ((1, 16),))
    up_weight = noise(keys[5], (D, EXPERTS * FF), D ** -0.5, 0.09375, ((1, 16),))
    down_weight = noise(keys[6], (EXPERTS * FF, D), FF ** -0.5, 0.125, ((0, 16),))
    return {"tokens": tokens, "norm_gain": norm_gain, "route_scores": route_scores, "expert_ids": expert_ids, "gate_weight": gate_weight, "up_weight": up_weight, "down_weight": down_weight}


def reference(tokens, norm_gain, route_scores, expert_ids, gate_weight, up_weight, down_weight):
    stats = tokens.astype(jnp.float32)
    scale = lax.rsqrt(lax.optimization_barrier(jnp.mean(stats * stats, axis=1, keepdims=True)) + 1e-06)
    normed = (stats * scale * norm_gain[None, :]).astype(jnp.bfloat16)
    weights = 2.5 * route_scores / lax.optimization_barrier(jnp.sum(route_scores, axis=1, keepdims=True))
    width = tokens.shape[1]
    shard = EXPERTS * FF // (N_EP * N_HG)
    block = min(shard, FF)
    pieces = FF // block

    def one_expert(total, expert):
        start = expert * FF
        gate_cols = lax.dynamic_slice_in_dim(gate_weight, start, FF, 1)
        up_cols = lax.dynamic_slice_in_dim(up_weight, start, FF, 1)
        gate_val = jnp.dot(normed, gate_cols, preferred_element_type=jnp.float32)
        up_val = jnp.dot(normed, up_cols, preferred_element_type=jnp.float32)
        act = (jax.nn.silu(gate_val) * up_val).astype(jnp.bfloat16)
        down_rows = lax.dynamic_slice_in_dim(down_weight, start, FF, 0)
        partial_value = jnp.einsum('tnb,nbd->ntd', act.reshape(-1, pieces, block).astype(jnp.float32), down_rows.reshape(pieces, block, width).astype(jnp.float32)).astype(jnp.bfloat16)
        partial_value = lax.optimization_barrier(partial_value)
        expert_out = lax.optimization_barrier(jnp.sum(partial_value.astype(jnp.float32), axis=0))
        coef = lax.optimization_barrier(jnp.sum(jnp.where(expert_ids == expert, weights, jnp.zeros_like(weights)), axis=1))
        return (total + coef[:, None] * expert_out, None)
    moe, _ = lax.scan(one_expert, jnp.zeros((TOKENS, width), jnp.float32), jnp.arange(EXPERTS, dtype=jnp.int32))
    return (stats + moe).astype(jnp.bfloat16)
```

```python
import functools
import jax
import jax.numpy as jnp
from jax import lax
from jax.experimental import pallas as pl
from jax.experimental.pallas import tpu as pltpu
from jax.sharding import PartitionSpec as P

FF = 2048
ROUTE_SCALE = 2.5
NORM_EPS = 1e-06
MESH = pl.DeviceIdType.MESH


def loop(count, step):
    if count == 1:
        step(0)
        return

    def once(i, carry):
        step(i)
        return carry

    lax.fori_loop(0, count, once, 0)


def kernel(
    n_ep,
    n_hg,
    tokens_ref,
    gain_ref,
    scores_ref,
    ids_ref,
    gate_ref,
    up_ref,
    down_ref,
    out_ref,
    gathered,
    gain,
    normed,
    gate_buf,
    up_buf,
    act,
    down_buf,
    outgoing,
    incoming,
    coef,
    gate_sem,
    up_sem,
    down_sem,
    gain_sem,
    token_send,
    token_recv,
    part_send,
    part_recv,
):
    group = lax.axis_index("groups")
    me = lax.axis_index("ep")
    lane = lax.axis_index("hg")
    rows, width = tokens_ref.shape
    chunks, _, chunk = gate_buf.shape
    shard = chunks * chunk
    half = width // n_hg
    pieces, _, _, _, piece = outgoing.shape
    parts = pieces * n_hg

    def gate_copy(c):
        cols = pl.ds(pl.multiple_of(c * chunk, 128), chunk)
        return pltpu.make_async_copy(gate_ref.at[:, cols], gate_buf.at[c], gate_sem.at[c])

    def up_copy(c):
        cols = pl.ds(pl.multiple_of(c * chunk, 128), chunk)
        return pltpu.make_async_copy(up_ref.at[:, cols], up_buf.at[c], up_sem.at[c])

    def down_copy(q):
        side = (lane + n_hg - 1 - q % n_hg) % n_hg
        start = side * half + q // n_hg * piece
        cols = pl.ds(pl.multiple_of(start, 128), piece)
        return pltpu.make_async_copy(down_ref.at[:, cols], down_buf.at[q], down_sem.at[q])

    def start_in(c):
        gate_copy(c).start()
        up_copy(c).start()

    own = pltpu.make_async_copy(tokens_ref, gathered.at[me], token_recv)
    own.start()
    gain_copy = pltpu.make_async_copy(gain_ref, gain, gain_sem)
    gain_copy.start()
    loop(chunks, start_in)

    barrier = pltpu.get_barrier_semaphore()
    for r in range(n_hg):
        side = (lane + r) % n_hg

        def greet(d):
            peer = (me + d + (r == 0)) % n_ep
            pl.semaphore_signal(barrier, inc=1, device_id=(group, peer, side), device_id_type=MESH)

        loop(n_ep - (r == 0), greet)
    pl.semaphore_wait(barrier, n_ep * n_hg - 1)

    def send_tokens(d):
        pltpu.make_async_remote_copy(
            src_ref=tokens_ref,
            dst_ref=gathered.at[me],
            send_sem=token_send,
            recv_sem=token_recv,
            device_id=(group, (me + d + 1) % n_ep, lane),
            device_id_type=MESH,
        ).start()

    loop(n_ep - 1, send_tokens)
    loop(parts, lambda q: down_copy(q).start())

    scores = scores_ref[...]
    weights = ROUTE_SCALE * scores / jnp.sum(scores, axis=1, keepdims=True)
    chosen = ids_ref[...]

    def weigh(s):
        expert = s * shard // FF
        total = jnp.sum(jnp.where(chosen == expert, weights, 0.0), axis=1, keepdims=True)
        coef[s] = jnp.broadcast_to(total, (rows, 128))

    loop(n_ep * n_hg, weigh)

    gain_copy.wait()
    pltpu.make_async_copy(gathered, gathered, token_recv).wait()
    batch = 16 // rows

    def norm(i):
        stats = jnp.concatenate(
            [gathered[i * batch + b].astype(jnp.float32) for b in range(batch)], axis=0
        )
        scale = lax.rsqrt(jnp.mean(stats * stats, axis=1, keepdims=True) + NORM_EPS)
        rows_at = pl.ds(pl.multiple_of(i * 16, 16), 16)
        normed[rows_at, :] = (stats * scale * gain[...]).astype(jnp.bfloat16)

    loop(n_ep // batch, norm)

    def first(c):
        gate_copy(c).wait()
        up_copy(c).wait()
        gate_val = jnp.dot(normed[...], gate_buf[c], preferred_element_type=jnp.float32)
        up_val = jnp.dot(normed[...], up_buf[c], preferred_element_type=jnp.float32)
        value = gate_val / (1.0 + jnp.exp(-gate_val)) * up_val
        act[:, pl.ds(pl.multiple_of(c * chunk, 128), chunk)] = value.astype(jnp.bfloat16)

    loop(chunks, first)

    source = me * n_hg + lane

    def second(p):
        for r in reversed(range(n_hg)):
            side = (lane + r) % n_hg
            q = p * n_hg + n_hg - 1 - r
            down_copy(q).wait()
            value = jnp.dot(act[...], down_buf[q], preferred_element_type=jnp.float32)
            for j in range(n_ep):
                outgoing[p, r, j] = value[j * rows : (j + 1) * rows].astype(jnp.bfloat16)

            def send(d):
                peer = (me + d + (r == 0)) % n_ep
                pltpu.make_async_remote_copy(
                    src_ref=outgoing.at[p, r, peer],
                    dst_ref=incoming.at[p, source],
                    send_sem=part_send.at[p, r],
                    recv_sem=part_recv.at[p],
                    device_id=(group, peer, side),
                    device_id_type=MESH,
                ).start()

            loop(n_ep - (r == 0), send)
            if r == 0:
                pltpu.make_async_copy(
                    outgoing.at[p, r, me], incoming.at[p, source], part_recv.at[p]
                ).start()

    loop(pieces, second)

    def finish(p):
        here = incoming.at[p]
        pltpu.make_async_copy(here, here, part_recv.at[p]).wait()
        start = pl.multiple_of(lane * half + p * piece, 128)
        resid = gathered[me, :, pl.ds(start, piece)].astype(jnp.float32)

        def add(s, total):
            weight = jnp.concatenate([coef[s]] * (piece // 128), axis=1)
            return total + weight * incoming[p, s].astype(jnp.float32)

        moe = lax.fori_loop(
            0, n_ep * n_hg, add, jnp.zeros((rows, piece), jnp.float32), unroll=min(16, n_ep * n_hg)
        )
        cols = pl.ds(pl.multiple_of(p * piece, 128), piece)
        out_ref[:, cols] = (resid + moe).astype(jnp.bfloat16)

    loop(pieces, finish)

    rest = gathered.at[pl.ds(0, n_ep - 1)]
    pltpu.make_async_copy(rest, rest, token_send).wait()

    def drain(p):
        for r in range(n_hg):
            sent = outgoing.at[p, r, pl.ds(0, n_ep - (r == 0))]
            pltpu.make_async_copy(sent, sent, part_send.at[p, r]).wait()

    loop(pieces, drain)


def body(tokens, norm_gain, route_scores, expert_ids, gate_weight, up_weight, down_weight):
    n_ep = lax.axis_size("ep")
    n_hg = lax.axis_size("hg")
    rows, width = tokens.shape
    shard = gate_weight.shape[1]
    chunk = min(shard, 256)
    chunks = shard // chunk
    half = width // n_hg
    piece = 256
    pieces = half // piece
    total = rows * n_ep
    sources = n_ep * n_hg
    hbm = pl.BlockSpec(memory_space=pl.ANY)
    vmem = pl.BlockSpec(memory_space=pltpu.VMEM)
    dma = pltpu.SemaphoreType.DMA
    return pl.pallas_call(
        functools.partial(kernel, n_ep, n_hg),
        out_shape=jax.ShapeDtypeStruct((rows, half), jnp.bfloat16),
        in_specs=[hbm, hbm, vmem, vmem, hbm, hbm, hbm],
        out_specs=vmem,
        scratch_shapes=[
            pltpu.VMEM((n_ep, rows, width), jnp.bfloat16),
            pltpu.VMEM((1, width), jnp.float32),
            pltpu.VMEM((total, width), jnp.bfloat16),
            pltpu.VMEM((chunks, width, chunk), jnp.bfloat16),
            pltpu.VMEM((chunks, width, chunk), jnp.bfloat16),
            pltpu.VMEM((total, shard), jnp.bfloat16),
            pltpu.VMEM((pieces * n_hg, shard, piece), jnp.bfloat16),
            pltpu.VMEM((pieces, n_hg, n_ep, rows, piece), jnp.bfloat16),
            pltpu.VMEM((pieces, sources, rows, piece), jnp.bfloat16),
            pltpu.VMEM((sources, rows, 128), jnp.float32),
            dma((chunks,)),
            dma((chunks,)),
            dma((pieces * n_hg,)),
            dma,
            dma,
            dma,
            dma((pieces, n_hg)),
            dma((pieces,)),
        ],
        compiler_params=pltpu.CompilerParams(
            collective_id=0, has_side_effects=True, vmem_limit_bytes=56 * 1024 * 1024
        ),
    )(
        tokens,
        norm_gain.reshape(1, width),
        route_scores,
        expert_ids,
        gate_weight,
        up_weight,
        down_weight,
    )


def solution(mesh):
    return jax.shard_map(
        body,
        mesh=mesh,
        in_specs=(
            P(("groups", "ep"), None),
            P(),
            P(("groups", "ep"), None),
            P(("groups", "ep"), None),
            P(None, ("ep", "hg")),
            P(None, ("ep", "hg")),
            P(("ep", "hg"), None),
        ),
        out_specs=P(("groups", "ep"), "hg"),
        check_vma=False,
    )
```

```python
import functools
import jax
import jax.numpy as jnp
from jax import lax
from jax.experimental import pallas as pl
from jax.experimental.pallas import tpu as pltpu
from jax.sharding import PartitionSpec as P

FF = 2048
ROUTE_SCALE = 2.5
NORM_EPS = 1e-06
MESH = pl.DeviceIdType.MESH


def loop(count, step):
    if count == 1:
        step(0)
        return

    def once(i, carry):
        step(i)
        return carry

    lax.fori_loop(0, count, once, 0)


def kernel(
    n_ep,
    n_hg,
    tokens_ref,
    gain_ref,
    scores_ref,
    ids_ref,
    gate_ref,
    up_ref,
    down_ref,
    out_ref,
    tokens,
    gain,
    gathered,
    normed,
    gate_buf,
    up_buf,
    gate_sum,
    up_sum,
    act,
    down_buf,
    outgoing,
    incoming,
    coef,
    gate_sem,
    up_sem,
    down_sem,
    own_sem,
    row_send,
    row_recv,
    side_send,
    side_recv,
    part_send,
    part_recv,
):
    group = lax.axis_index("groups")
    me = lax.axis_index("ep")
    lane = lax.axis_index("hg")
    rows, width = tokens_ref.shape
    _, chunks, half, chunk = gate_buf.shape
    shard = chunks * chunk
    pieces, _, _, _, piece = outgoing.shape
    batch = 16 // rows

    barrier = pltpu.get_barrier_semaphore()
    for r in range(n_hg):
        side = (lane + r) % n_hg

        def greet(d):
            peer = (me + d + (r == 0)) % n_ep
            pl.semaphore_signal(barrier, inc=1, device_id=(group, peer, side), device_id_type=MESH)

        loop(n_ep - (r == 0), greet)

    own = pltpu.make_async_copy(tokens_ref, tokens, own_sem.at[0])
    own.start()
    gain_copy = pltpu.make_async_copy(gain_ref, gain.at[0], own_sem.at[1])
    gain_copy.start()

    def first_copy(source, target, sem, r, c):
        k = pl.ds(pl.multiple_of((lane + r) % n_hg * half, 256), half)
        cols = pl.ds(pl.multiple_of(c * chunk, 128), chunk)
        return pltpu.make_async_copy(source.at[k, cols], target.at[r, c], sem.at[r, c])

    def gate_copy(r, c):
        return first_copy(gate_ref, gate_buf, gate_sem, r, c)

    def up_copy(r, c):
        return first_copy(up_ref, up_buf, up_sem, r, c)

    def down_copy(p, r):
        start = (lane + r) % n_hg * half + p * piece
        cols = pl.ds(pl.multiple_of(start, 128), piece)
        return pltpu.make_async_copy(down_ref.at[:, cols], down_buf.at[p, r], down_sem.at[p, r])

    for r in range(n_hg):

        def start_first(c):
            gate_copy(r, c).start()
            up_copy(r, c).start()

        loop(chunks, start_first)

    def start_down(p):
        for r in reversed(range(n_hg)):
            down_copy(p, r).start()

    loop(pieces, start_down)

    own.wait()
    gain_copy.wait()
    own_half = pl.ds(pl.multiple_of(lane * half, 256), half)
    stats = tokens[...].astype(jnp.float32)
    scale = lax.rsqrt(jnp.mean(stats * stats, axis=1, keepdims=True) + NORM_EPS)
    stats = tokens[:, own_half].astype(jnp.float32)
    gathered[0, me] = (stats * scale * gain[:, own_half]).astype(jnp.bfloat16)

    scores = scores_ref[...]
    weights = ROUTE_SCALE * scores / jnp.sum(scores, axis=1, keepdims=True)
    chosen = ids_ref[...]

    def weigh(s):
        expert = s * shard // FF
        total = jnp.sum(jnp.where(chosen == expert, weights, 0.0), axis=1, keepdims=True)
        coef[s] = jnp.broadcast_to(total, (rows, 128))

    loop(n_ep * n_hg, weigh)

    pl.semaphore_wait(barrier, n_ep * n_hg - 1)

    def send_rows(d):
        pltpu.make_async_remote_copy(
            src_ref=gathered.at[0, me],
            dst_ref=gathered.at[0, me],
            send_sem=row_send,
            recv_sem=row_recv,
            device_id=(group, (me + d + 1) % n_ep, lane),
            device_id_type=MESH,
        ).start()

    loop(n_ep - 1, send_rows)
    others = gathered.at[0, pl.ds(0, n_ep - 1)]
    pltpu.make_async_copy(others, others, row_recv).wait()
    forwards = [
        pltpu.make_async_remote_copy(
            src_ref=gathered.at[0],
            dst_ref=gathered.at[r],
            send_sem=side_send.at[r - 1],
            recv_sem=side_recv.at[r - 1],
            device_id=(group, me, (lane + n_hg - r) % n_hg),
            device_id_type=MESH,
        )
        for r in range(1, n_hg)
    ]
    for forward in forwards:
        forward.start()

    for r in range(n_hg):
        if r > 0:
            forwards[r - 1].wait_recv()

        def lay(i):
            stacked = jnp.concatenate(
                [gathered[r, i * batch + b].astype(jnp.float32) for b in range(batch)], axis=0
            )
            normed[r, pl.ds(pl.multiple_of(i * 16, 16), 16), :] = stacked.astype(jnp.bfloat16)

        loop(n_ep // batch, lay)

        def first(c):
            gate_copy(r, c).wait()
            up_copy(r, c).wait()
            gate_val = jnp.dot(normed[r], gate_buf[r, c], preferred_element_type=jnp.float32)
            up_val = jnp.dot(normed[r], up_buf[r, c], preferred_element_type=jnp.float32)
            if r > 0:
                gate_val = gate_sum[c] + gate_val
                up_val = up_sum[c] + up_val
            if r < n_hg - 1:
                gate_sum[c] = gate_val
                up_sum[c] = up_val
            else:
                value = gate_val / (1.0 + jnp.exp(-gate_val)) * up_val
                cols = pl.ds(pl.multiple_of(c * chunk, 128), chunk)
                act[:, cols] = value.astype(jnp.bfloat16)

        loop(chunks, first)

    source = me * n_hg + lane

    def second(p):
        for r in reversed(range(n_hg)):
            side = (lane + r) % n_hg
            down_copy(p, r).wait()
            value = jnp.dot(act[...], down_buf[p, r], preferred_element_type=jnp.float32)
            for j in range(n_ep):
                outgoing[p, r, j] = value[j * rows : (j + 1) * rows].astype(jnp.bfloat16)

            def send(d):
                peer = (me + d + (r == 0)) % n_ep
                pltpu.make_async_remote_copy(
                    src_ref=outgoing.at[p, r, peer],
                    dst_ref=incoming.at[p, source],
                    send_sem=part_send.at[p, r],
                    recv_sem=part_recv.at[p],
                    device_id=(group, peer, side),
                    device_id_type=MESH,
                ).start()

            loop(n_ep - (r == 0), send)
            if r == 0:
                pltpu.make_async_copy(
                    outgoing.at[p, r, me], incoming.at[p, source], part_recv.at[p]
                ).start()

    loop(pieces, second)

    def finish(p):
        here = incoming.at[p]
        pltpu.make_async_copy(here, here, part_recv.at[p]).wait()
        start = pl.multiple_of(lane * half + p * piece, 128)
        resid = tokens[:, pl.ds(start, piece)].astype(jnp.float32)

        def add(s, total):
            weight = jnp.concatenate([coef[s]] * (piece // 128), axis=1)
            return total + weight * incoming[p, s].astype(jnp.float32)

        moe = lax.fori_loop(
            0, n_ep * n_hg, add, jnp.zeros((rows, piece), jnp.float32), unroll=min(16, n_ep * n_hg)
        )
        cols = pl.ds(pl.multiple_of(p * piece, 128), piece)
        out_ref[:, cols] = resid + moe

    loop(pieces, finish)

    pltpu.make_async_copy(others, others, row_send).wait()
    for forward in forwards:
        forward.wait_send()

    def drain(p):
        for r in range(n_hg):
            sent = outgoing.at[p, r, pl.ds(0, n_ep - (r == 0))]
            pltpu.make_async_copy(sent, sent, part_send.at[p, r]).wait()

    loop(pieces, drain)


def body(tokens, norm_gain, route_scores, expert_ids, gate_weight, up_weight, down_weight):
    n_ep = lax.axis_size("ep")
    n_hg = lax.axis_size("hg")
    rows, width = tokens.shape
    shard = gate_weight.shape[1]
    chunk = min(shard, 512)
    chunks = shard // chunk
    half = width // n_hg
    pieces = 2
    piece = half // pieces
    total = rows * n_ep
    sources = n_ep * n_hg
    hbm = pl.BlockSpec(memory_space=pl.ANY)
    vmem = pl.BlockSpec(memory_space=pltpu.VMEM)
    dma = pltpu.SemaphoreType.DMA
    mixed = pl.pallas_call(
        functools.partial(kernel, n_ep, n_hg),
        out_shape=jax.ShapeDtypeStruct((rows, half), jnp.float32),
        in_specs=[hbm, hbm, vmem, vmem, hbm, hbm, hbm],
        out_specs=vmem,
        scratch_shapes=[
            pltpu.VMEM((rows, width), jnp.bfloat16),
            pltpu.VMEM((1, width), jnp.float32),
            pltpu.VMEM((n_hg, n_ep, rows, half), jnp.bfloat16),
            pltpu.VMEM((n_hg, total, half), jnp.bfloat16),
            pltpu.VMEM((n_hg, chunks, half, chunk), jnp.bfloat16),
            pltpu.VMEM((n_hg, chunks, half, chunk), jnp.bfloat16),
            pltpu.VMEM((chunks, total, chunk), jnp.float32),
            pltpu.VMEM((chunks, total, chunk), jnp.float32),
            pltpu.VMEM((total, shard), jnp.bfloat16),
            pltpu.VMEM((pieces, n_hg, shard, piece), jnp.bfloat16),
            pltpu.VMEM((pieces, n_hg, n_ep, rows, piece), jnp.bfloat16),
            pltpu.VMEM((pieces, sources, rows, piece), jnp.bfloat16),
            pltpu.VMEM((sources, rows, 128), jnp.float32),
            dma((n_hg, chunks)),
            dma((n_hg, chunks)),
            dma((pieces, n_hg)),
            dma((2,)),
            dma,
            dma,
            dma((n_hg - 1,)),
            dma((n_hg - 1,)),
            dma((pieces, n_hg)),
            dma((pieces,)),
        ],
        compiler_params=pltpu.CompilerParams(
            collective_id=0, has_side_effects=True, vmem_limit_bytes=56 * 1024 * 1024
        ),
    )(tokens, norm_gain, route_scores, expert_ids, gate_weight, up_weight, down_weight)
    return mixed.astype(jnp.bfloat16)


def solution(mesh):
    return jax.shard_map(
        body,
        mesh=mesh,
        in_specs=(
            P(("groups", "ep"), None),
            P(),
            P(("groups", "ep"), None),
            P(("groups", "ep"), None),
            P(None, ("ep", "hg")),
            P(None, ("ep", "hg")),
            P(("ep", "hg"), None),
        ),
        out_specs=P(("groups", "ep"), "hg"),
        check_vma=False,
    )
```

```python
import functools
import jax
import jax.numpy as jnp
from jax import lax
from jax.experimental import pallas as pl
from jax.experimental.pallas import tpu as pltpu
from jax.sharding import PartitionSpec as P

FF = 2048
ROUTE_SCALE = 2.5
NORM_EPS = 1e-06
MESH = pl.DeviceIdType.MESH


def loop(count, step):
    if count == 1:
        step(0)
        return

    def once(i, carry):
        step(i)
        return carry

    lax.fori_loop(0, count, once, 0)


def kernel(
    n_ep,
    n_hg,
    tokens_ref,
    gain_ref,
    scores_ref,
    ids_ref,
    gate_ref,
    up_ref,
    down_ref,
    out_ref,
    tokens,
    gain,
    gathered,
    normed,
    gate_buf,
    up_buf,
    gate_sum,
    up_sum,
    act,
    down_buf,
    hand_out,
    hand_in,
    outgoing,
    incoming,
    coef,
    gate_sem,
    up_sem,
    down_sem,
    own_sem,
    row_send,
    row_recv,
    side_send,
    side_recv,
    coef_send,
    coef_recv,
    hand_send,
    hand_recv,
    part_send,
    part_recv,
):
    group = lax.axis_index("groups")
    me = lax.axis_index("ep")
    lane = lax.axis_index("hg")
    rows, width = tokens_ref.shape
    _, chunks, half, chunk = gate_buf.shape
    shard = chunks * chunk
    pieces, _, _, piece = outgoing.shape
    batch = 16 // rows

    barrier = pltpu.get_barrier_semaphore()

    def greet(d):
        peer = (me + d + 1) % n_ep
        pl.semaphore_signal(barrier, inc=1, device_id=(group, peer, lane), device_id_type=MESH)

    loop(n_ep - 1, greet)
    for r in range(1, n_hg):
        side = (lane + r) % n_hg
        pl.semaphore_signal(barrier, inc=1, device_id=(group, me, side), device_id_type=MESH)

    own = pltpu.make_async_copy(tokens_ref, tokens, own_sem.at[0])
    own.start()
    gain_copy = pltpu.make_async_copy(gain_ref, gain.at[0], own_sem.at[1])
    gain_copy.start()

    def first_copy(source, target, sem, r, c):
        k = pl.ds(pl.multiple_of((lane + r) % n_hg * half, 256), half)
        cols = pl.ds(pl.multiple_of(c * chunk, 128), chunk)
        return pltpu.make_async_copy(source.at[k, cols], target.at[r, c], sem.at[r, c])

    def gate_copy(r, c):
        return first_copy(gate_ref, gate_buf, gate_sem, r, c)

    def up_copy(r, c):
        return first_copy(up_ref, up_buf, up_sem, r, c)

    def down_copy(p, r):
        start = (lane + r) % n_hg * half + p * piece
        cols = pl.ds(pl.multiple_of(start, 128), piece)
        return pltpu.make_async_copy(down_ref.at[:, cols], down_buf.at[p, r], down_sem.at[p, r])

    for r in range(n_hg):

        def start_first(c):
            gate_copy(r, c).start()
            up_copy(r, c).start()

        loop(chunks, start_first)

    for r in reversed(range(n_hg)):
        loop(pieces, lambda p: down_copy(p, r).start())

    own.wait()
    gain_copy.wait()
    own_half = pl.ds(pl.multiple_of(lane * half, 256), half)
    stats = tokens[...].astype(jnp.float32)
    scale = lax.rsqrt(jnp.mean(stats * stats, axis=1, keepdims=True) + NORM_EPS)
    stats = tokens[:, own_half].astype(jnp.float32)
    gathered[0, me] = (stats * scale * gain[:, own_half]).astype(jnp.bfloat16)

    scores = scores_ref[...]
    weights = ROUTE_SCALE * scores / jnp.sum(scores, axis=1, keepdims=True)
    chosen = ids_ref[...]

    expert = lax.broadcasted_iota(jnp.int32, (rows, 128), 1)
    total = jnp.zeros((rows, 128), jnp.float32)
    for k in range(scores.shape[1]):
        total = total + jnp.where(chosen[:, k : k + 1] == expert, weights[:, k : k + 1], 0.0)
    coef[me] = total

    pl.semaphore_wait(barrier, n_ep + n_hg - 2)

    def send_rows(d):
        pltpu.make_async_remote_copy(
            src_ref=gathered.at[0, me],
            dst_ref=gathered.at[0, me],
            send_sem=row_send,
            recv_sem=row_recv,
            device_id=(group, (me + d + 1) % n_ep, lane),
            device_id_type=MESH,
        ).start()

    loop(n_ep - 1, send_rows)

    def send_coef(d):
        pltpu.make_async_remote_copy(
            src_ref=coef.at[me],
            dst_ref=coef.at[me],
            send_sem=coef_send,
            recv_sem=coef_recv,
            device_id=(group, (me + d + 1) % n_ep, lane),
            device_id_type=MESH,
        ).start()

    loop(n_ep - 1, send_coef)
    others = gathered.at[0, pl.ds(0, n_ep - 1)]
    pltpu.make_async_copy(others, others, row_recv).wait()
    forwards = [
        pltpu.make_async_remote_copy(
            src_ref=gathered.at[0],
            dst_ref=gathered.at[r],
            send_sem=side_send.at[r - 1],
            recv_sem=side_recv.at[r - 1],
            device_id=(group, me, (lane + n_hg - r) % n_hg),
            device_id_type=MESH,
        )
        for r in range(1, n_hg)
    ]
    for forward in forwards:
        forward.start()

    for r in range(n_hg):
        if r > 0:
            forwards[r - 1].wait_recv()

        def lay(i):
            stacked = jnp.concatenate(
                [gathered[r, i * batch + b].astype(jnp.float32) for b in range(batch)], axis=0
            )
            normed[r, pl.ds(pl.multiple_of(i * 16, 16), 16), :] = stacked.astype(jnp.bfloat16)

        loop(n_ep // batch, lay)

        def first(c):
            gate_copy(r, c).wait()
            up_copy(r, c).wait()
            gate_val = jnp.dot(normed[r], gate_buf[r, c], preferred_element_type=jnp.float32)
            up_val = jnp.dot(normed[r], up_buf[r, c], preferred_element_type=jnp.float32)
            if r > 0:
                gate_val = gate_sum[c] + gate_val
                up_val = up_sum[c] + up_val
            if r < n_hg - 1:
                gate_sum[c] = gate_val
                up_sum[c] = up_val
            else:
                value = gate_val / (1.0 + jnp.exp(-gate_val)) * up_val
                cols = pl.ds(pl.multiple_of(c * chunk, 128), chunk)
                act[:, cols] = value.astype(jnp.bfloat16)

        loop(chunks, first)

    other_coefs = coef.at[pl.ds(0, n_ep - 1)]
    pltpu.make_async_copy(other_coefs, other_coefs, coef_recv).wait()
    held = (me * n_hg + lane) * shard // FF
    column = lax.broadcasted_iota(jnp.int32, (rows * n_ep, 128), 1)
    every = jnp.concatenate([coef[j] for j in range(n_ep)], axis=0)
    weight = jnp.sum(jnp.where(column == held, every, 0.0), axis=1, keepdims=True)

    def second(p, r):
        down_copy(p, r).wait()
        return weight * jnp.dot(act[...], down_buf[p, r], preferred_element_type=jnp.float32)

    def hand(p, r):
        return pltpu.make_async_remote_copy(
            src_ref=hand_out.at[p, r - 1],
            dst_ref=hand_in.at[p, r - 1],
            send_sem=hand_send.at[p, r - 1],
            recv_sem=hand_recv.at[p, r - 1],
            device_id=(group, me, (lane + r) % n_hg),
            device_id_type=MESH,
        )

    for r in range(1, n_hg):

        def give(p):
            hand_out[p, r - 1] = second(p, r).astype(jnp.bfloat16)
            hand(p, r).start()

        loop(pieces, give)

    def send_back(p):
        value = second(p, 0)
        for r in range(1, n_hg):
            hand(p, r).wait_recv()
            value = value + hand_in[p, r - 1].astype(jnp.float32)
        for j in range(n_ep):
            outgoing[p, j] = value[j * rows : (j + 1) * rows].astype(jnp.bfloat16)

        def send(d):
            peer = (me + d + 1) % n_ep
            pltpu.make_async_remote_copy(
                src_ref=outgoing.at[p, peer],
                dst_ref=incoming.at[p, me],
                send_sem=part_send.at[p],
                recv_sem=part_recv.at[p],
                device_id=(group, peer, lane),
                device_id_type=MESH,
            ).start()

        loop(n_ep - 1, send)
        pltpu.make_async_copy(outgoing.at[p, me], incoming.at[p, me], part_recv.at[p]).start()

    loop(pieces, send_back)

    def finish(p):
        here = incoming.at[p]
        pltpu.make_async_copy(here, here, part_recv.at[p]).wait()
        start = pl.multiple_of(lane * half + p * piece, 128)
        total = tokens[:, pl.ds(start, piece)].astype(jnp.float32)

        def add(s, total):
            return total + incoming[p, s].astype(jnp.float32)

        total = lax.fori_loop(0, n_ep, add, total, unroll=min(8, n_ep))
        cols = pl.ds(pl.multiple_of(p * piece, 128), piece)
        out_ref[:, cols] = total

    loop(pieces, finish)

    pltpu.make_async_copy(others, others, row_send).wait()
    for forward in forwards:
        forward.wait_send()

    pltpu.make_async_copy(other_coefs, other_coefs, coef_send).wait()

    def drain(p):
        for r in range(1, n_hg):
            hand(p, r).wait_send()
        sent = outgoing.at[p, pl.ds(0, n_ep - 1)]
        pltpu.make_async_copy(sent, sent, part_send.at[p]).wait()

    loop(pieces, drain)


def body(tokens, norm_gain, route_scores, expert_ids, gate_weight, up_weight, down_weight):
    n_ep = lax.axis_size("ep")
    n_hg = lax.axis_size("hg")
    rows, width = tokens.shape
    shard = gate_weight.shape[1]
    chunk = min(shard, 512)
    chunks = shard // chunk
    half = width // n_hg
    pieces = 2
    piece = half // pieces
    total = rows * n_ep
    hbm = pl.BlockSpec(memory_space=pl.ANY)
    vmem = pl.BlockSpec(memory_space=pltpu.VMEM)
    dma = pltpu.SemaphoreType.DMA
    mixed = pl.pallas_call(
        functools.partial(kernel, n_ep, n_hg),
        out_shape=pltpu.VMEM((rows, half), jnp.float32),
        in_specs=[hbm, hbm, vmem, vmem, hbm, hbm, hbm],
        out_specs=vmem,
        scratch_shapes=[
            pltpu.VMEM((rows, width), jnp.bfloat16),
            pltpu.VMEM((1, width), jnp.float32),
            pltpu.VMEM((n_hg, n_ep, rows, half), jnp.bfloat16),
            pltpu.VMEM((n_hg, total, half), jnp.bfloat16),
            pltpu.VMEM((n_hg, chunks, half, chunk), jnp.bfloat16),
            pltpu.VMEM((n_hg, chunks, half, chunk), jnp.bfloat16),
            pltpu.VMEM((chunks, total, chunk), jnp.float32),
            pltpu.VMEM((chunks, total, chunk), jnp.float32),
            pltpu.VMEM((total, shard), jnp.bfloat16),
            pltpu.VMEM((pieces, n_hg, shard, piece), jnp.bfloat16),
            pltpu.VMEM((pieces, n_hg - 1, total, piece), jnp.bfloat16),
            pltpu.VMEM((pieces, n_hg - 1, total, piece), jnp.bfloat16),
            pltpu.VMEM((pieces, n_ep, rows, piece), jnp.bfloat16),
            pltpu.VMEM((pieces, n_ep, rows, piece), jnp.bfloat16),
            pltpu.VMEM((n_ep, rows, 128), jnp.float32),
            dma((n_hg, chunks)),
            dma((n_hg, chunks)),
            dma((pieces, n_hg)),
            dma((2,)),
            dma,
            dma,
            dma((n_hg - 1,)),
            dma((n_hg - 1,)),
            dma,
            dma,
            dma((pieces, n_hg - 1)),
            dma((pieces, n_hg - 1)),
            dma((pieces,)),
            dma((pieces,)),
        ],
        compiler_params=pltpu.CompilerParams(
            collective_id=0, has_side_effects=True, vmem_limit_bytes=56 * 1024 * 1024
        ),
    )(tokens, norm_gain, route_scores, expert_ids, gate_weight, up_weight, down_weight)
    return mixed.astype(jnp.bfloat16)


def solution(mesh):
    return jax.shard_map(
        body,
        mesh=mesh,
        in_specs=(
            P(("groups", "ep"), None),
            P(),
            P(("groups", "ep"), None),
            P(("groups", "ep"), None),
            P(None, ("ep", "hg")),
            P(None, ("ep", "hg")),
            P(("ep", "hg"), None),
        ),
        out_specs=P(("groups", "ep"), "hg"),
        check_vma=False,
    )
```
